512 devices in a mesh: vocab: 32 (over x, z), dp: 16 (over y, core).
Axes of the slice: x: 4, y: 8, z: 8, core: 2. Of those that a mesh axis runs over, the one named last changes fastest.
Arguments:
- ex_hidden: bfloat16 [128, 7168], P('dp'), may hold values from -72 to 72
- ex_target: int32 [128], P('dp'), may hold values from 0 to 129279
- q_hidden: bfloat16 [128, 7168], P('dp'), may hold values from -72 to 72
- q_target: int32 [128], P('dp'), may hold values from 0 to 129279
- head: bfloat16 [129280, 7168], P('vocab', 'dp'), may hold values from -0.25 to 0.25
- out_proj: bfloat16 [129280, 64], P('vocab'), may hold values from -2 to 2
- in_proj: bfloat16 [7168, 64], P('vocab'), may hold values from -0.0234375 to 0.0234375
Outputs:
- scores: float32 [128, 128], P('dp')
The draws below stay inside these ranges and needn't reach their ends.
All inputs are finite; a program needn't handle non-finite values.
Results may differ from the reference program's by a relative error of at most 0.0012.
Values may be sent and summed in bfloat16 or wider, within the bound.
A program may use at most 64 MiB of HBM per device.

```python
import jax
import jax.numpy as jnp
from jax import lax

D = 7168
V = 129280
KP = 64
EXAMPLES = 128
QUERIES = 128


def draw_ex_hidden(key, part):
    key = jax.random.fold_in(key, 11)
    first = jax.random.fold_in(key, 0)
    base = jnp.clip(jax.random.normal(first, (EXAMPLES, D), jnp.float32), -6.0, 6.0)
    return base.astype(jnp.bfloat16)


def draw_q_hidden(key, part):
    key = jax.random.fold_in(key, 23)
    first = jax.random.fold_in(key, 0)
    base = jnp.clip(jax.random.normal(first, (QUERIES, D), jnp.float32), -6.0, 6.0)
    return base.astype(jnp.bfloat16)


def set_ends(entries, own_key, low, top_value):
    longest = entries.shape.index(max(entries.shape))
    spots = []
    for shift in (0, 1):
        where = [jax.random.randint(jax.random.fold_in(own_key, axis), (), 0, length) for axis, length in enumerate(entries.shape)]
        where[longest] = (where[longest] + shift) % entries.shape[longest]
        spots.append(tuple(where))
    return entries.at[spots[0]].set(low).at[spots[1]].set(top_value)


def level_of(own_key, shape, cuts, least, largest):
    level = 1.0
    for dim, parts in cuts:
        steps = jax.random.uniform(jax.random.fold_in(jax.random.fold_in(own_key, 6), dim), (parts,), jnp.float32, least / len(cuts), largest / len(cuts))
        level = level * jnp.repeat(jnp.exp(steps), shape[dim] // parts).reshape((-1,) + (1,) * (len(shape) - 1 - dim))
    return level


def bell_draw(rng, shape, width, bound, shards=(), kind=jnp.bfloat16):
    drawn = width * jax.random.normal(rng, shape, jnp.float32)
    if shards:
        drawn = drawn * level_of(rng, shape, shards, -0.22, 0.18)
    return jnp.clip(drawn, -bound, bound).astype(kind)


def setup_inputs(seed: int = 0) -> dict:
    splits = jax.random.split(jax.random.key(seed), 8)
    return {
        "ex_hidden": draw_ex_hidden(jax.random.fold_in(splits[7], 71), 0),
        "ex_target": set_ends(jax.random.randint(splits[1], (EXAMPLES,), 0, V), jax.random.fold_in(splits[1], 1), 0, V - 1).astype(jnp.int32),
        "q_hidden": draw_q_hidden(jax.random.fold_in(splits[7], 71), 0),
        "q_target": set_ends(jax.random.randint(splits[3], (QUERIES,), 0, V), jax.random.fold_in(splits[3], 1), 0, V - 1).astype(jnp.int32),
        "head": bell_draw(splits[4], (V, D), (D // 16) ** -0.5, 0.25, ((0, 32), (1, 16))),
        "out_proj": bell_draw(splits[5], (V, KP), 8 ** -0.5, 2.0, ((0, 32),)),
        "in_proj": bell_draw(splits[6], (D, KP), (8 * D) ** -0.5, 0.0234375, ((0, 32),)),
    }


def reference(ex_hidden, ex_target, q_hidden, q_target, head, out_proj, in_proj):
    stacked = jnp.concatenate([ex_hidden, q_hidden], 0)
    targets = jnp.concatenate([ex_target, q_target], 0).astype(jnp.int32)
    blocks = head.reshape(64, V // 64, D)

    def block_logits(block):
        return jnp.dot(stacked, block.T, preferred_element_type=jnp.float32)

    logits = lax.map(block_logits, blocks)
    logits = jnp.transpose(logits, (1, 0, 2)).reshape(stacked.shape[0], V)
    prob = jax.nn.softmax(logits, axis=1)
    columns = lax.broadcasted_iota(jnp.int32, (1, V), 1)
    onehot = (columns == targets[:, None]).astype(prob.dtype)
    resid = (prob - onehot).astype(jnp.bfloat16)
    a_proj = jnp.dot(resid, out_proj, preferred_element_type=jnp.float32)
    b_proj = jnp.dot(stacked, in_proj, preferred_element_type=jnp.float32)
    left = jnp.dot(a_proj[:EXAMPLES], a_proj[EXAMPLES:].T, precision=lax.Precision.HIGHEST)
    right = jnp.dot(b_proj[:EXAMPLES], b_proj[EXAMPLES:].T, precision=lax.Precision.HIGHEST)
    return left * right
```

```python
import functools

import jax
import jax.numpy as jnp
from jax import lax
from jax.experimental import pallas as pl
from jax.experimental.pallas import tpu as pltpu
from jax.sharding import PartitionSpec as P

MESH = pl.DeviceIdType.MESH
NT = (((1,), (1,)), ((), ()))
CHIPS = 8
CORES = 2
NX, NZ = 4, 8
ROWS = 8
VOCAB = 4040
PAD = 4096
COLS = 448
KP = 64
TILE = 512
HALVES = 2
HALF = PAD // HALVES
F32 = jnp.float32
BF16 = jnp.bfloat16


def kernel(
    ex_hbm, ext_hbm, q_hbm, qt_hbm, head_hbm, out_hbm, in_hbm,
    scores_ref,
    ex_v, q_v, head_v, outp_v, inp_v, ext_s, qt_s,
    xs, xbuf, pbuf, sbuf, obuf, rbuf, wz,
    early_own, early_z, early_x, late_own, late_z, late_x, late_mid, early_mid,
    qbuf,
    load_sem, a2a_send, a2a_recv, sib_send, sib_recv, ring_send, ring_recv,
    ez_send, ez_recv, ex_send, ex_recv, lz_send, lz_recv, lx_send, lx_recv, q_send, q_recv,
):
    dp = lax.axis_index("dp")
    voc = lax.axis_index("vocab")
    y, core = dp // CORES, dp % CORES
    x, z = voc // NZ, voc % NZ
    sib = 1 - core

    def dp_of(chip, c):
        return lax.rem(chip + 2 * CHIPS, CHIPS) * CORES + c

    dp_partners = [dp_of(y + rc, c) for rc in range(CHIPS) for c in (core, sib)][1:]
    z_partners = [x * NZ + lax.rem(z + r, NZ) for r in range(1, NZ)]
    x_partners = [lax.rem(x + r, NX) * NZ + z for r in range(1, NX)]

    barrier = pltpu.get_barrier_semaphore()
    for d in dp_partners:
        pl.semaphore_signal(barrier, inc=1, device_id={"dp": d}, device_id_type=MESH)
    for d in z_partners + x_partners:
        pl.semaphore_signal(barrier, inc=1, device_id={"vocab": d}, device_id_type=MESH)

    loads = [
        pltpu.make_async_copy(src, dst, load_sem.at[i])
        for i, (src, dst) in enumerate(
            [(ex_hbm, ex_v), (q_hbm, q_v), (head_hbm, head_v), (ext_hbm, ext_s), (qt_hbm, qt_s), (out_hbm, outp_v), (in_hbm, inp_v)]
        )
    ]
    for c in loads:
        c.start()
    sends = []

    def push(src, dst, ssem, rsem, target):
        c = pltpu.make_async_remote_copy(
            src_ref=src, dst_ref=dst, send_sem=ssem, recv_sem=rsem, device_id=target, device_id_type=MESH
        )
        c.start()
        sends.append(c)
        return c

    loads[0].wait()
    loads[1].wait()
    for j in range(CHIPS * CORES):
        cut = pl.ds(COLS * j, COLS)
        block = jnp.concatenate([ex_v[:, cut].astype(F32), q_v[:, cut].astype(F32)], 0)
        xs[j] = block.astype(BF16)
    xbuf[0, 0] = xs[dp]

    pl.semaphore_wait(barrier, len(dp_partners) + len(z_partners) + len(x_partners))

    a2a = {}
    for rc in (1, 7, 2, 6, 3, 5, 4, 0):
        for k, c in enumerate((core, sib)):
            if rc == 0 and k == 0:
                continue
            t = dp_of(y + rc, c)
            a2a[rc, k] = push(
                xs.at[t], xbuf.at[rc, k], a2a_send.at[rc * 2 + k], a2a_recv.at[rc * 2 + k], {"dp": t}
            )

    for i in (3, 4, 5, 6):
        loads[i].wait()
    row = lax.broadcasted_iota(jnp.int32, (2 * ROWS, 1), 0)
    tcol = jnp.zeros((2 * ROWS, 1), jnp.int32)
    for r in range(ROWS):
        tcol = jnp.where(row == r, ext_s[r], tcol)
        tcol = jnp.where(row == ROWS + r, qt_s[r], tcol)
    tcol = tcol - voc * VOCAB
    hot = (lax.broadcasted_iota(jnp.int32, (2 * ROWS, VOCAB), 1) == tcol).astype(F32).astype(BF16)
    t_part = jnp.dot(hot, outp_v[...], preferred_element_type=F32)
    wz[...] = jnp.zeros_like(wz)
    depth = inp_v.shape[0]
    wz[pl.ds(pl.multiple_of(depth * lax.rem(voc, 2), 16), depth), :] = inp_v[...]
    b_part = jnp.dot(xs[voc // 2], wz[...], preferred_element_type=F32)
    early_own[...] = jnp.concatenate([t_part, b_part], 1)
    ez = [
        push(early_own, early_z.at[r], ez_send.at[r], ez_recv.at[r], {"vocab": t}) for r, t in enumerate(z_partners)
    ]

    loads[2].wait()

    def logits(rcs):
        for rc in rcs:
            for k in range(2):
                if (rc, k) in a2a:
                    a2a[rc, k].wait_recv()
        rows = jnp.concatenate([xbuf[rc, k] for rc in rcs for k in range(2)], 0)
        for n in range(0, PAD, TILE):
            width = min(TILE, VOCAB - n)
            part = lax.dot_general(rows, head_v[n:n + width, :], NT, preferred_element_type=F32)
            i = 0
            for rc in rcs:
                for k in range(2):
                    pbuf[rc, k, :, n:n + width] = part[i:i + 2 * ROWS]
                    i += 2 * ROWS
        for rc in rcs:
            for k in range(2):
                pbuf[rc, k, :, VOCAB:PAD] = jnp.zeros((2 * ROWS, PAD - VOCAB), F32)
            twin[rc] = push(
                pbuf.at[rc, 1], sbuf.at[rc], sib_send.at[rc], sib_recv.at[rc], {"dp": dp_of(y, sib)}
            )

    twin = {}
    waited = set()
    ring = {}

    def chip_sum(direction, rc, half):
        rows = pl.ds(ROWS * direction, ROWS)
        lanes = pl.ds(HALF * half, HALF)
        if rc not in waited:
            twin[rc].wait_recv()
            waited.add(rc)
        return pbuf[rc, 0, rows, lanes] + sbuf[rc, rows, lanes]

    def ring_step(s):
        for half in range(HALVES):
            lanes = pl.ds(HALF * half, HALF)
            for direction in range(2):
                rc = 1 + s if direction == 0 else 7 - s
                total = chip_sum(direction, rc, half)
                if s:
                    ring[direction, s - 1, half].wait_recv()
                    total = total + rbuf[direction, s - 1, :, lanes]
                obuf[direction, s, :, lanes] = total
                i = (direction * 7 + s) * HALVES + half
                to = dp_of(y + 1, core) if direction == 0 else dp_of(y - 1, core)
                ring[direction, s, half] = push(
                    obuf.at[direction, s, :, lanes], rbuf.at[direction, s, :, lanes],
                    ring_send.at[i], ring_recv.at[i], {"dp": to},
                )

    logits((1, 7))
    ring_step(0)
    logits((2, 6))
    ring_step(1)
    logits((3, 5))
    ring_step(2)
    logits((4, 0))
    ring_step(3)

    for c in ez:
        c.wait_recv()
    mid = early_own[...]
    for r in range(NZ - 1):
        mid = mid + early_z[r]
    early_mid[...] = mid
    exs = [
        push(early_mid, early_x.at[r], ex_send.at[r], ex_recv.at[r], {"vocab": t}) for r, t in enumerate(x_partners)
    ]
    ring_step(4)
    ring_step(5)
    for c in exs:
        c.wait_recv()
    for r in range(NX - 1):
        mid = mid + early_x[r]
    ring_step(6)

    own = []
    for half in range(HALVES):
        for direction in range(2):
            ring[direction, 6, half].wait_recv()
    for direction in range(2):
        rows = pl.ds(ROWS * direction, ROWS)
        own.append(pbuf[0, 0, rows, :VOCAB] + (sbuf_wait(twin, waited, sbuf, rows)) + rbuf[direction, 6, :, :VOCAB])
    full = jnp.concatenate(own, 0)
    top = jnp.max(full, axis=1, keepdims=True)
    e = jnp.exp(full - top)
    mass = jnp.sum(e, axis=1, keepdims=True)
    hi = e.astype(BF16)
    lo = (e - hi.astype(F32)).astype(BF16)
    num = jnp.dot(jnp.concatenate([hi, lo], 0), outp_v[...], preferred_element_type=F32)
    num = num[:2 * ROWS] + num[2 * ROWS:]
    quarter = (2 * ROWS, KP // 2)
    late_own[...] = jnp.concatenate([num, jnp.broadcast_to(top, quarter), jnp.broadcast_to(mass, quarter)], 1)

    lane = lax.broadcasted_iota(jnp.int32, (2 * ROWS, 2 * KP), 1)
    is_top = (lane >= KP) & (lane < KP + KP // 2)

    def merge(parts):
        tops = [p[:, KP:KP + 1] for p in parts]
        best = functools.reduce(jnp.maximum, tops)
        total = sum(p * jnp.exp(t - best) for p, t in zip(parts, tops))
        return jnp.where(is_top, best, total)

    lz = [push(late_own, late_z.at[r], lz_send.at[r], lz_recv.at[r], {"vocab": t}) for r, t in enumerate(z_partners)]
    for c in lz:
        c.wait_recv()
    merged = merge([late_own[...]] + [late_z[r] for r in range(NZ - 1)])
    late_mid[...] = merged
    lx = [push(late_mid, late_x.at[r], lx_send.at[r], lx_recv.at[r], {"vocab": t}) for r, t in enumerate(x_partners)]
    for c in lx:
        c.wait_recv()
    merged = merge([merged] + [late_x[r] for r in range(NX - 1)])
    a_proj = merged[:, :KP] / merged[:, 2 * KP - 1:] - mid[:, :KP]
    factors = jnp.concatenate([a_proj, mid[:, KP:]], 1)
    qbuf[dp] = factors[ROWS:]
    qs = []
    for r in range(1, CHIPS * CORES):
        qs.append(push(qbuf.at[dp], qbuf.at[dp], q_send.at[r], q_recv.at[r], {"dp": lax.rem(dp + r, CHIPS * CORES)}))
    mine = factors[:ROWS]
    zero = jnp.zeros((ROWS, KP), F32)
    both = jnp.concatenate(
        [jnp.concatenate([mine[:, :KP], zero], 1), jnp.concatenate([zero, mine[:, KP:]], 1)], 0
    )
    for c in qs:
        c.wait_recv()
    queries = qbuf[...].reshape(CHIPS * CORES * ROWS, 2 * KP)
    inner = lax.dot_general(both, queries, NT, precision=lax.Precision.HIGHEST, preferred_element_type=F32)
    scores_ref[...] = inner[:ROWS] * inner[ROWS:]
    for c in sends:
        c.wait_send()


def sbuf_wait(twin, waited, sbuf, rows):
    if 0 not in waited:
        twin[0].wait_recv()
        waited.add(0)
    return sbuf[0, rows, :VOCAB]


def body(ex_hidden, ex_target, q_hidden, q_target, head, out_proj, in_proj):
    dma = pltpu.SemaphoreType.DMA
    vm = pltpu.VMEM
    two = 2 * ROWS
    scratch = [
        vm(ex_hidden.shape, BF16), vm(q_hidden.shape, BF16), vm(head.shape, BF16), vm(out_proj.shape, BF16),
        vm(in_proj.shape, BF16), pltpu.SMEM((ROWS,), jnp.int32), pltpu.SMEM((ROWS,), jnp.int32),
        vm((CHIPS * CORES, two, COLS), BF16), vm((CHIPS, 2, two, COLS), BF16),
        vm((CHIPS, 2, two, PAD), F32), vm((CHIPS, two, PAD), F32),
        vm((2, CHIPS - 1, ROWS, PAD), F32), vm((2, CHIPS - 1, ROWS, PAD), F32), vm((COLS, KP), BF16),
        vm((two, 2 * KP), F32), vm((NZ - 1, two, 2 * KP), F32), vm((NX - 1, two, 2 * KP), F32),
        vm((two, 2 * KP), F32), vm((NZ - 1, two, 2 * KP), F32), vm((NX - 1, two, 2 * KP), F32),
        vm((two, 2 * KP), F32), vm((two, 2 * KP), F32),
        vm((CHIPS * CORES, ROWS, 2 * KP), F32),
        dma((7,)), dma((16,)), dma((16,)), dma((8,)), dma((8,)), dma((14 * HALVES,)), dma((14 * HALVES,)),
        dma((7,)), dma((7,)), dma((3,)), dma((3,)), dma((7,)), dma((7,)), dma((3,)), dma((3,)), dma((16,)), dma((16,)),
    ]
    return pl.pallas_call(
        kernel,
        out_shape=jax.ShapeDtypeStruct((ROWS, CHIPS * CORES * ROWS), F32),
        in_specs=[pl.BlockSpec(memory_space=pl.ANY)] * 7,
        out_specs=pl.BlockSpec(memory_space=pltpu.VMEM),
        scratch_shapes=scratch,
        compiler_params=pltpu.CompilerParams(
            collective_id=0, has_side_effects=True, vmem_limit_bytes=40 * 1024 * 1024
        ),
    )(ex_hidden, ex_target, q_hidden, q_target, head, out_proj, in_proj)


def solution(mesh):
    in_specs = (
        P("dp", None),
        P("dp"),
        P("dp", None),
        P("dp"),
        P("vocab", "dp"),
        P("vocab", None),
        P("vocab", None),
    )
    return jax.shard_map(body, mesh=mesh, in_specs=in_specs, out_specs=P("dp", None), check_vma=False)
```
